32 devices in a mesh: expert: 8 (over z, x), panel: 4 (over y, core).
Axes of the slice: x: 2, y: 2, z: 4, core: 2. Of those that a mesh axis runs over, the one named last changes fastest.
Arguments:
- lower_factor: bfloat16 [28672, 3584], P(('expert', 'panel')), parts along dimension 0, may hold values from -1 to 2.5, as said below
- inverses: float32 [128, 224, 224], P(('expert', 'panel')), parts along dimension 0, may hold values from -1 to 1.3, as said below
- probes: bfloat16 [28672, 512], P(('expert', 'panel')), parts along dimension 0, may hold values from -6 to 6
Outputs:
- whitened: float32 [28672, 512], P(('expert', 'panel')), parts along dimension 0
The draws below stay inside these ranges and needn't reach their ends.
There are 8 independent parts, one for each index of `expert`. The reference program is written for one: setup_inputs(seed, part) draws one part's arguments, and reference() takes and returns one part's arrays. A program takes and returns all parts, laid end to end along the dimension named above; each array names one. Nothing has to cross between parts.
Inputs may be any that keep to these rules, and one draw needn't show every extreme that they name: lower_factor is lower triangular with a positive diagonal. inverses[b] is lower triangular, the inverse of the b-th diagonal 224 x 224 block of lower_factor up to float32 rounding.
All inputs are finite; a program needn't handle non-finite values.
Results may differ from the reference program's by a relative error of at most 0.0011.
Values may be sent and summed in bfloat16 or wider, within the bound.
A program may use at most 64 MiB of HBM per device.

```python
import jax
import jax.numpy as jnp
from jax import lax

D = 3584
COLUMNS = 512
BLOCK = 224
NBLOCKS = 16


def make_factor(key):
    first_key, second_key = jax.random.split(jax.random.fold_in(key, 7))
    diagonal = jnp.exp(jax.random.uniform(first_key, (D,), jnp.float32, 0.0, 0.7))
    off_part = jax.random.truncated_normal(second_key, -4.0, 4.0, (D, D), jnp.float32)
    whole = jnp.tril(off_part * (0.7 / jnp.sqrt(D * 1.0)), -1) + jnp.diag(diagonal)
    return whole.astype(jnp.bfloat16).astype(jnp.float32)


def draw_lower_factor(key, part):
    return make_factor(key).astype(jnp.bfloat16)


def draw_inverses(key, part):
    whole = make_factor(key)
    tiles = whole.reshape(NBLOCKS, BLOCK, NBLOCKS, BLOCK)
    picks = jnp.arange(NBLOCKS)
    diagonal_blocks = tiles[picks, :, picks, :]
    identity = jnp.eye(BLOCK, dtype=jnp.float32)
    invert = lambda tile: jax.scipy.linalg.solve_triangular(tile, identity, lower=True)
    return jax.vmap(invert)(diagonal_blocks).astype(jnp.float32)


def levels(rng, dims, pieces, smallest, high):
    factor_of = 1.0
    for dim, shards_of in pieces:
        draws = jax.random.uniform(jax.random.fold_in(jax.random.fold_in(rng, 6), dim), (shards_of,), jnp.float32, smallest / len(pieces), high / len(pieces))
        factor_of = factor_of * jnp.repeat(jnp.exp(draws), dims[dim] // shards_of).reshape((-1,) + (1,) * (len(dims) - 1 - dim))
    return factor_of


def noise(key, dims, width, most, cuts=(), kind=jnp.bfloat16):
    level = levels(key, dims, cuts, -0.22, 0.18) if cuts else 1.0
    drawn = jax.random.normal(key, dims, jnp.float32) * width * level
    return jnp.minimum(jnp.maximum(drawn, -most), most).astype(kind)


def setup_inputs(seed: int = 0, part: int = 0) -> dict:
    key_list = jax.random.split(jax.random.key(seed), 4)
    part_keys = jax.random.split(jax.random.fold_in(key_list[3], part), 4)
    lower_factor = draw_lower_factor(jax.random.fold_in(jax.random.fold_in(key_list[3], part), 71), part)
    inverses = draw_inverses(jax.random.fold_in(jax.random.fold_in(key_list[3], part), 71), part)
    probes = noise(part_keys[2], (D, COLUMNS), 1.0, 6.0, ((0, 4),))
    return {"lower_factor": lower_factor, "inverses": inverses, "probes": probes}


def reference(lower_factor, inverses, probes):
    outputs = []
    halves = []
    for block_index in range(NBLOCKS):
        first = block_index * BLOCK
        residual = probes[first:first + BLOCK].astype(jnp.float32)
        if block_index > 0:
            earlier = jnp.concatenate(halves, 0)
            residual = residual - jnp.dot(lower_factor[first:first + BLOCK, :first].astype(jnp.float32), earlier.astype(jnp.float32), preferred_element_type=jnp.float32)
        solved = jnp.dot(inverses[block_index].astype(jnp.float32), residual.astype(jnp.float32), precision=lax.Precision.HIGHEST, preferred_element_type=jnp.float32)
        outputs.append(solved)
        halves.append(solved.astype(jnp.bfloat16))
    return jnp.concatenate(outputs, 0)
```

```python
import functools

import jax
import jax.numpy as jnp
from jax import lax
from jax.experimental import pallas as pl
from jax.experimental.pallas import tpu as pltpu
from jax.sharding import PartitionSpec as P

MESH = pl.DeviceIdType.MESH
WIDTH = 256


def dot(a, b):
    return jnp.dot(a, b, preferred_element_type=jnp.float32)


def split(x):
    high = x.astype(jnp.bfloat16)
    return high, (x - high.astype(jnp.float32)).astype(jnp.bfloat16)


def kernel(
    panels, width, flat, lower, inverses, probes, out,
    factor, inverse, inv_high, inv_low, probe, result, solved, pending,
    load_sem, factor_sem, send_sem, recv_sem, out_sem,
):
    count, size = inverses.shape[0], inverses.shape[1]
    rows = count * size
    chunks = probes.shape[1] // width
    me = lax.axis_index("panel")
    after = lax.rem(me + 1, panels)
    has_next = me < panels - 1

    barrier = pltpu.get_barrier_semaphore()

    @pl.when(me > 0)
    def _():
        pl.semaphore_signal(barrier, inc=1, device_id={"panel": me - 1}, device_id_type=MESH)

    def load_factor(q):
        if flat:
            source = lower.at[:, pl.ds(pl.multiple_of(q * rows, 128), rows)]
        else:
            source = lower.at[q]
        return pltpu.make_async_copy(source, factor.at[q], factor_sem.at[q])

    load_inverse = pltpu.make_async_copy(inverses, inverse, load_sem.at[0])
    load_probe = pltpu.make_async_copy(probes, probe, load_sem.at[1])
    load_inverse.start()
    load_probe.start()
    load_factor(me).start()

    def start_factor(q, carry):
        load_factor(q).start()
        return carry

    lax.fori_loop(0, me, start_factor, 0)

    for c in range(chunks):
        solved[c, pl.ds(pl.multiple_of(me * rows, 16), rows)] = jnp.zeros((rows, width), jnp.bfloat16)
    load_inverse.wait()
    for b in range(count):
        inv_high[b], inv_low[b] = split(inverse[b])
    load_probe.wait()
    load_factor(me).wait()

    @pl.when(has_next)
    def _():
        pl.semaphore_wait(barrier, 1)

    def block_copy(c, g):
        block = solved.at[c, pl.ds(pl.multiple_of(g * size, 16), size)]
        return pltpu.make_async_remote_copy(
            src_ref=block,
            dst_ref=block,
            send_sem=send_sem.at[c, g],
            recv_sem=recv_sem.at[c, g],
            device_id={"panel": after},
            device_id_type=MESH,
        )

    def send(c, g):
        @pl.when(has_next)
        def _():
            block_copy(c, g).start()

    def out_copy(c):
        columns = pl.ds(pl.multiple_of(c * width, 128), width)
        return pltpu.make_async_copy(result.at[:, columns], out.at[:, columns], out_sem.at[c])

    def chunk(c, carry):
        columns = pl.ds(pl.multiple_of(c * width, 128), width)
        pending[...] = probe[:, columns].astype(jnp.float32)

        def earlier(q, carry):
            @pl.when(c == 0)
            def _():
                load_factor(q).wait()

            for j in range(count):
                block_copy(c, q * count + j).wait_recv()
                send(c, q * count + j)
            there = pl.ds(pl.multiple_of(q * rows, 16), rows)
            pending[...] -= dot(factor[q], solved[c, there])
            return carry

        lax.fori_loop(0, me, earlier, 0)

        for b in range(count):
            here = slice(b * size, (b + 1) * size)
            residual = pending[here]
            if b > 0:
                depth = min(rows, -(-b * size // 256) * 256)
                own = pl.ds(pl.multiple_of(me * rows, 16), depth)
                residual = residual - dot(factor[me, here, :depth], solved[c, own])
            high, low = split(residual)
            block = dot(inv_high[b], high) + (dot(inv_high[b], low) + dot(inv_low[b], high))
            result[here, columns] = block
            g = me * count + b
            solved[c, pl.ds(pl.multiple_of(g * size, 16), size)] = block.astype(jnp.bfloat16)
            send(c, g)
        out_copy(c).start()
        return carry

    lax.fori_loop(0, chunks, chunk, 0)

    def finish(c, carry):
        out_copy(c).wait()

        @pl.when(has_next)
        def _():
            def sent(g, carry):
                block_copy(c, g).wait_send()
                return carry

            lax.fori_loop(0, (me + 1) * count, sent, 0)

        return carry

    lax.fori_loop(0, chunks, finish, 0)


def per_device(lower_factor, inverses, probes):
    panels = lax.axis_size("panel")
    count, size, _ = inverses.shape
    rows, columns = probes.shape
    width = WIDTH if columns % WIDTH == 0 else columns
    chunks = columns // width
    flat = rows % 128 == 0
    if not flat:
        lower_factor = lower_factor.reshape(rows, panels, rows).transpose(1, 0, 2)
    bf16, f32 = jnp.bfloat16, jnp.float32
    dma = pltpu.SemaphoreType.DMA
    return pl.pallas_call(
        functools.partial(kernel, panels, width, flat),
        out_shape=jax.ShapeDtypeStruct((rows, columns), f32),
        in_specs=[pl.BlockSpec(memory_space=pl.ANY)] * 3,
        out_specs=pl.BlockSpec(memory_space=pl.ANY),
        scratch_shapes=[
            pltpu.VMEM((panels, rows, rows), bf16),
            pltpu.VMEM((count, size, size), f32),
            pltpu.VMEM((count, size, size), bf16),
            pltpu.VMEM((count, size, size), bf16),
            pltpu.VMEM((rows, columns), bf16),
            pltpu.VMEM((rows, columns), f32),
            pltpu.VMEM((chunks, panels * rows, width), bf16),
            pltpu.VMEM((rows, width), f32),
            dma((2,)),
            dma((panels,)),
            dma((chunks, panels * count)),
            dma((chunks, panels * count)),
            dma((chunks,)),
        ],
        compiler_params=pltpu.CompilerParams(
            collective_id=0, has_side_effects=True, vmem_limit_bytes=48 * 1024 * 1024
        ),
    )(lower_factor, inverses, probes)


def solution(mesh):
    return jax.shard_map(
        per_device,
        mesh=mesh,
        in_specs=(
            P(("expert", "panel"), None),
            P(("expert", "panel"), None, None),
            P(("expert", "panel"), None),
        ),
        out_specs=P(("expert", "panel"), None),
        check_vma=False,
    )
```

```python
import functools

import jax
import jax.numpy as jnp
from jax import lax
from jax.experimental import pallas as pl
from jax.experimental.pallas import tpu as pltpu
from jax.sharding import PartitionSpec as P

MESH = pl.DeviceIdType.MESH
WIDTH = 256


def dot(a, b):
    return jnp.dot(a, b, preferred_element_type=jnp.float32)


def split(x):
    high = x.astype(jnp.bfloat16)
    return high, (x - high.astype(jnp.float32)).astype(jnp.bfloat16)


def kernel(
    panels, width, flat, lower, inverses, probes, out,
    factor, inverse, inv_high, inv_low, fold_high, fold_low, probe, result, solved, pending,
    load_sem, factor_sem, send_sem, recv_sem, out_sem,
):
    count, size = inverses.shape[0], inverses.shape[1]
    rows = count * size
    chunks = probes.shape[1] // width
    me = lax.axis_index("panel")
    after = lax.rem(me + 1, panels)
    has_next = me < panels - 1
    blocks = [slice(b * size, (b + 1) * size) for b in range(count)]

    barrier = pltpu.get_barrier_semaphore()

    @pl.when(me > 0)
    def _():
        pl.semaphore_signal(barrier, inc=1, device_id={"panel": me - 1}, device_id_type=MESH)

    def load_factor(q):
        if flat:
            source = lower.at[:, pl.ds(pl.multiple_of(q * rows, 128), rows)]
        else:
            source = lower.at[q]
        return pltpu.make_async_copy(source, factor.at[q], factor_sem.at[q])

    def block_copy(c, g):
        block = solved.at[c, pl.ds(pl.multiple_of(g * size, 16), size)]
        return pltpu.make_async_remote_copy(
            src_ref=block,
            dst_ref=block,
            send_sem=send_sem.at[c, g],
            recv_sem=recv_sem.at[c, g],
            device_id={"panel": after},
            device_id_type=MESH,
        )

    def send(c, g):
        @pl.when(has_next)
        def _():
            block_copy(c, g).start()

    def columns_of(c):
        return pl.ds(pl.multiple_of(c * width, 128), width)

    def out_copy(c, b):
        return pltpu.make_async_copy(
            result.at[blocks[b], columns_of(c)], out.at[blocks[b], columns_of(c)], out_sem.at[c, b]
        )

    def begin(c):
        for b in range(count):
            given = probe[blocks[b], columns_of(c)]
            pending[blocks[b]] = dot(inv_high[b], given) + dot(inv_low[b], given)

    def fold(q, j, first):
        for b in range(first, count):
            part = factor[q, blocks[b], blocks[j]]
            g = q * count + j
            fold_high[g, blocks[b]], fold_low[g, blocks[b]] = split(
                dot(inv_high[b], part) + dot(inv_low[b], part)
            )

    def update(c, g, first):
        block = solved[c, pl.ds(pl.multiple_of(g * size, 16), size)]
        below = slice(first * size, rows)
        pending[below] -= dot(fold_high[g, below], block) + dot(fold_low[g, below], block)

    def finalize(c, b):
        block = pending[blocks[b]]
        g = me * count + b
        solved[c, pl.ds(pl.multiple_of(g * size, 16), size)] = block.astype(jnp.bfloat16)
        send(c, g)
        result[blocks[b], columns_of(c)] = block
        out_copy(c, b).start()

    load_inverse = pltpu.make_async_copy(inverses, inverse, load_sem.at[0])
    load_probe = pltpu.make_async_copy(probes, probe, load_sem.at[1])
    load_inverse.start()
    load_probe.start()
    load_factor(me).start()

    def start_factor(q, carry):
        load_factor(q).start()
        return carry

    lax.fori_loop(0, me, start_factor, 0)
    load_inverse.wait()
    for b in range(count):
        inv_high[b], inv_low[b] = split(inverse[b])
    load_probe.wait()
    begin(0)

    @pl.when(has_next)
    def _():
        pl.semaphore_wait(barrier, 1)

    @pl.when(me == 0)
    def _():
        finalize(0, 0)

    load_factor(me).wait()
    for j in range(count - 1):
        fold(me, j, j + 1)

    def chunk(c, carry):
        @pl.when(c > 0)
        def _():
            begin(c)

        def earlier(q, carry):
            @pl.when(c == 0)
            def _():
                load_factor(q).wait()

            for j in range(count):
                g = q * count + j
                block_copy(c, g).wait_recv()
                send(c, g)

                @pl.when(c == 0)
                def _():
                    fold(q, j, 0)

                update(c, g, 0)
            return carry

        lax.fori_loop(0, me, earlier, 0)

        @pl.when(me + c > 0)
        def _():
            finalize(c, 0)

        for b in range(1, count):
            update(c, me * count + b - 1, b)
            finalize(c, b)
        return carry

    lax.fori_loop(0, chunks, chunk, 0)

    def finish(c, carry):
        for b in range(count):
            out_copy(c, b).wait()

        @pl.when(has_next)
        def _():
            def sent(g, carry):
                block_copy(c, g).wait_send()
                return carry

            lax.fori_loop(0, (me + 1) * count, sent, 0)

        return carry

    lax.fori_loop(0, chunks, finish, 0)


def per_device(lower_factor, inverses, probes):
    panels = lax.axis_size("panel")
    count, size, _ = inverses.shape
    rows, columns = probes.shape
    width = WIDTH if columns % WIDTH == 0 else columns
    chunks = columns // width
    flat = rows % 128 == 0
    if not flat:
        lower_factor = lower_factor.reshape(rows, panels, rows).transpose(1, 0, 2)
    bf16, f32 = jnp.bfloat16, jnp.float32
    dma = pltpu.SemaphoreType.DMA
    return pl.pallas_call(
        functools.partial(kernel, panels, width, flat),
        out_shape=jax.ShapeDtypeStruct((rows, columns), f32),
        in_specs=[pl.BlockSpec(memory_space=pltpu.HBM)] * 3,
        out_specs=pl.BlockSpec(memory_space=pl.ANY),
        scratch_shapes=[
            pltpu.VMEM((panels, rows, rows), bf16),
            pltpu.VMEM((count, size, size), f32),
            pltpu.VMEM((count, size, size), bf16),
            pltpu.VMEM((count, size, size), bf16),
            pltpu.VMEM((panels * count, rows, size), bf16),
            pltpu.VMEM((panels * count, rows, size), bf16),
            pltpu.VMEM((rows, columns), bf16),
            pltpu.VMEM((rows, columns), f32),
            pltpu.VMEM((chunks, panels * rows, width), bf16),
            pltpu.VMEM((rows, width), f32),
            dma((2,)),
            dma((panels,)),
            dma((chunks, panels * count)),
            dma((chunks, panels * count)),
            dma((chunks, count)),
        ],
        compiler_params=pltpu.CompilerParams(
            collective_id=0, has_side_effects=True, vmem_limit_bytes=48 * 1024 * 1024
        ),
    )(lower_factor, inverses, probes)


def solution(mesh):
    return jax.shard_map(
        per_device,
        mesh=mesh,
        in_specs=(
            P(("expert", "panel"), None),
            P(("expert", "panel"), None, None),
            P(("expert", "panel"), None),
        ),
        out_specs=P(("expert", "panel"), None),
        check_vma=False,
    )
```

```python
import functools

import jax
import jax.numpy as jnp
from jax import lax
from jax.experimental import pallas as pl
from jax.experimental.pallas import tpu as pltpu
from jax.sharding import PartitionSpec as P

MESH = pl.DeviceIdType.MESH
WIDTH = 256


def dot(a, b):
    return jnp.dot(a, b, preferred_element_type=jnp.float32)


def split(x):
    high = x.astype(jnp.bfloat16)
    return high, (x - high.astype(jnp.float32)).astype(jnp.bfloat16)


def kernel(
    panels, width, flat, lower, inverses, probes, out,
    factor, inverse, inv_high, inv_low, folded, probe, result, solved, pending,
    load_sem, factor_sem, send_sem, recv_sem, out_sem,
):
    count, size = inverses.shape[0], inverses.shape[1]
    rows = count * size
    chunks = probes.shape[1] // width
    me = lax.axis_index("panel")
    after = lax.rem(me + 1, panels)
    has_next = me < panels - 1
    blocks = [slice(b * size, (b + 1) * size) for b in range(count)]

    barrier = pltpu.get_barrier_semaphore()

    @pl.when(me > 0)
    def _():
        pl.semaphore_signal(barrier, inc=1, device_id={"panel": me - 1}, device_id_type=MESH)

    def load_factor(q):
        if flat:
            source = lower.at[:, pl.ds(pl.multiple_of(q * rows, 128), rows)]
        else:
            source = lower.at[q]
        return pltpu.make_async_copy(source, factor.at[q], factor_sem.at[q])

    def block_copy(c, g):
        block = solved.at[c, pl.ds(pl.multiple_of(g * size, 16), size)]
        return pltpu.make_async_remote_copy(
            src_ref=block,
            dst_ref=block,
            send_sem=send_sem.at[c, g],
            recv_sem=recv_sem.at[c, g],
            device_id={"panel": after},
            device_id_type=MESH,
        )

    def send(c, g):
        @pl.when(has_next)
        def _():
            block_copy(c, g).start()

    def columns_of(c):
        return pl.ds(pl.multiple_of(c * width, 128), width)

    def out_copy(c, b):
        return pltpu.make_async_copy(
            result.at[blocks[b], columns_of(c)], out.at[blocks[b], columns_of(c)], out_sem.at[c, b]
        )

    def begin(c):
        for b in range(count):
            given = probe[blocks[b], columns_of(c)]
            pending[blocks[b]] = dot(inv_high[b], given) + dot(inv_low[b], given)

    def fold(q, j, first):
        for b in range(first, count):
            part = factor[q, blocks[b], blocks[j]]
            g = q * count + j
            folded[g, blocks[b]] = (dot(inv_high[b], part) + dot(inv_low[b], part)).astype(jnp.bfloat16)

    def update(c, g, first):
        block = solved[c, pl.ds(pl.multiple_of(g * size, 16), size)]
        below = slice(first * size, rows)
        pending[below] -= dot(folded[g, below], block)

    def finalize(c, b):
        block = pending[blocks[b]]
        g = me * count + b
        solved[c, pl.ds(pl.multiple_of(g * size, 16), size)] = block.astype(jnp.bfloat16)
        send(c, g)
        result[blocks[b], columns_of(c)] = block
        out_copy(c, b).start()

    load_inverse = pltpu.make_async_copy(inverses, inverse, load_sem.at[0])
    load_probe = pltpu.make_async_copy(probes, probe, load_sem.at[1])
    load_inverse.start()
    load_probe.start()
    load_factor(me).start()

    def start_factor(q, carry):
        load_factor(q).start()
        return carry

    lax.fori_loop(0, me, start_factor, 0)
    load_inverse.wait()
    for b in range(count):
        inv_high[b], inv_low[b] = split(inverse[b])
    load_probe.wait()
    begin(0)

    @pl.when(has_next)
    def _():
        pl.semaphore_wait(barrier, 1)

    @pl.when(me == 0)
    def _():
        finalize(0, 0)

    load_factor(me).wait()
    for j in range(count - 1):
        fold(me, j, j + 1)

    def chunk(c, carry):
        @pl.when(c > 0)
        def _():
            begin(c)

        def earlier(q, carry):
            @pl.when(c == 0)
            def _():
                load_factor(q).wait()

            for j in range(count):
                g = q * count + j
                block_copy(c, g).wait_recv()
                send(c, g)

                @pl.when(c == 0)
                def _():
                    fold(q, j, 0)

                update(c, g, 0)
            return carry

        lax.fori_loop(0, me, earlier, 0)

        @pl.when(me + c > 0)
        def _():
            finalize(c, 0)

        for b in range(1, count):
            update(c, me * count + b - 1, b)
            finalize(c, b)
        return carry

    lax.fori_loop(0, chunks, chunk, 0)

    def finish(c, carry):
        for b in range(count):
            out_copy(c, b).wait()

        @pl.when(has_next)
        def _():
            def sent(g, carry):
                block_copy(c, g).wait_send()
                return carry

            lax.fori_loop(0, (me + 1) * count, sent, 0)

        return carry

    lax.fori_loop(0, chunks, finish, 0)


def per_device(lower_factor, inverses, probes):
    panels = lax.axis_size("panel")
    count, size, _ = inverses.shape
    rows, columns = probes.shape
    width = WIDTH if columns % WIDTH == 0 else columns
    chunks = columns // width
    flat = rows % 128 == 0
    if not flat:
        lower_factor = lower_factor.reshape(rows, panels, rows).transpose(1, 0, 2)
    bf16, f32 = jnp.bfloat16, jnp.float32
    dma = pltpu.SemaphoreType.DMA
    return pl.pallas_call(
        functools.partial(kernel, panels, width, flat),
        out_shape=pltpu.VMEM((rows, columns), f32),
        in_specs=[pl.BlockSpec(memory_space=pltpu.HBM)] * 3,
        out_specs=pl.BlockSpec(memory_space=pl.ANY),
        scratch_shapes=[
            pltpu.VMEM((panels, rows, rows), bf16),
            pltpu.VMEM((count, size, size), f32),
            pltpu.VMEM((count, size, size), bf16),
            pltpu.VMEM((count, size, size), bf16),
            pltpu.VMEM((panels * count, rows, size), bf16),
            pltpu.VMEM((rows, columns), bf16),
            pltpu.VMEM((rows, columns), f32),
            pltpu.VMEM((chunks, panels * rows, width), bf16),
            pltpu.VMEM((rows, width), f32),
            dma((2,)),
            dma((panels,)),
            dma((chunks, panels * count)),
            dma((chunks, panels * count)),
            dma((chunks, count)),
        ],
        compiler_params=pltpu.CompilerParams(
            collective_id=0, has_side_effects=True, vmem_limit_bytes=54 * 1024 * 1024
        ),
    )(lower_factor, inverses, probes)


def solution(mesh):
    return jax.shard_map(
        per_device,
        mesh=mesh,
        in_specs=(
            P(("expert", "panel"), None),
            P(("expert", "panel"), None, None),
            P(("expert", "panel"), None),
        ),
        out_specs=P(("expert", "panel"), None),
        check_vma=False,
    )
```

```python
import functools

import jax
import jax.numpy as jnp
from jax import lax
from jax.experimental import pallas as pl
from jax.experimental.pallas import tpu as pltpu
from jax.sharding import PartitionSpec as P

MESH = pl.DeviceIdType.MESH
WIDTH = 256


def dot(a, b):
    return jnp.dot(a, b, preferred_element_type=jnp.float32)


def split(x):
    high = x.astype(jnp.bfloat16)
    return high, (x - high.astype(jnp.float32)).astype(jnp.bfloat16)


def kernel(
    panels, width, flat, lower, inverses, probes, out,
    factor, inverse, inv_high, inv_low, fold_high, fold_low, probe, solved, pending,
    load_sem, factor_sem, send_sem, recv_sem,
):
    count, size = inverses.shape[0], inverses.shape[1]
    rows = count * size
    chunks = probes.shape[1] // width
    me = lax.axis_index("panel")
    after = lax.rem(me + 1, panels)
    has_next = me < panels - 1
    blocks = [slice(b * size, (b + 1) * size) for b in range(count)]

    barrier = pltpu.get_barrier_semaphore()

    @pl.when(me > 0)
    def _():
        pl.semaphore_signal(barrier, inc=1, device_id={"panel": me - 1}, device_id_type=MESH)

    def load_factor(q):
        if flat:
            source = lower.at[:, pl.ds(pl.multiple_of(q * rows, 128), rows)]
        else:
            source = lower.at[q]
        return pltpu.make_async_copy(source, factor.at[q], factor_sem.at[q])

    def block_copy(c, g):
        block = solved.at[c, pl.ds(pl.multiple_of(g * size, 16), size)]
        return pltpu.make_async_remote_copy(
            src_ref=block,
            dst_ref=block,
            send_sem=send_sem.at[c, g],
            recv_sem=recv_sem.at[c, g],
            device_id={"panel": after},
            device_id_type=MESH,
        )

    def send(c, g):
        @pl.when(has_next)
        def _():
            block_copy(c, g).start()

    def columns_of(c):
        return pl.ds(pl.multiple_of(c * width, 128), width)

    def begin(c):
        for b in range(count):
            given = probe[blocks[b], columns_of(c)]
            pending[blocks[b]] = dot(inv_high[b], given) + dot(inv_low[b], given)

    def in_two(j, first):
        return first == 0 and (j < count - 1 or count == 1)

    def fold(q, j, first):
        for b in range(first, count):
            part = factor[q, blocks[b], blocks[j]]
            g = q * count + j
            high, low = split(dot(inv_high[b], part) + dot(inv_low[b], part))
            fold_high[g, blocks[b]] = high
            if in_two(j, first):
                fold_low[g, blocks[b]] = low

    def update(c, g, first, two=False):
        block = solved[c, pl.ds(pl.multiple_of(g * size, 16), size)]
        below = slice(first * size, rows)
        change = dot(fold_high[g, below], block)
        if two:
            change += dot(fold_low[g, below], block)
        pending[below] -= change

    def finalize(c, b):
        block = pending[blocks[b]]
        g = me * count + b
        solved[c, pl.ds(pl.multiple_of(g * size, 16), size)] = block.astype(jnp.bfloat16)
        send(c, g)
        out[blocks[b], columns_of(c)] = block

    load_inverse = pltpu.make_async_copy(inverses, inverse, load_sem.at[0])
    load_probe = pltpu.make_async_copy(probes, probe, load_sem.at[1])
    load_inverse.start()
    load_probe.start()
    load_factor(me).start()

    def start_factor(q, carry):
        load_factor(q).start()
        return carry

    lax.fori_loop(0, me, start_factor, 0)
    load_inverse.wait()
    for b in range(count):
        inv_high[b], inv_low[b] = split(inverse[b])
    load_probe.wait()
    begin(0)

    @pl.when(has_next)
    def _():
        pl.semaphore_wait(barrier, 1)

    @pl.when(me == 0)
    def _():
        finalize(0, 0)

    load_factor(me).wait()
    for j in range(count - 1):
        fold(me, j, j + 1)

    def chunk(c, carry):
        @pl.when(c > 0)
        def _():
            begin(c)

        def earlier(q, carry):
            @pl.when(c == 0)
            def _():
                load_factor(q).wait()

            for j in range(count):
                g = q * count + j
                block_copy(c, g).wait_recv()
                send(c, g)

                @pl.when(c == 0)
                def _():
                    fold(q, j, 0)

                update(c, g, 0, in_two(j, 0))
            return carry

        lax.fori_loop(0, me, earlier, 0)

        @pl.when(me + c > 0)
        def _():
            finalize(c, 0)

        for b in range(1, count):
            update(c, me * count + b - 1, b)
            finalize(c, b)
        return carry

    lax.fori_loop(0, chunks, chunk, 0)

    def finish(c, carry):
        @pl.when(has_next)
        def _():
            def sent(g, carry):
                block_copy(c, g).wait_send()
                return carry

            lax.fori_loop(0, (me + 1) * count, sent, 0)

        return carry

    lax.fori_loop(0, chunks, finish, 0)


def per_device(lower_factor, inverses, probes):
    panels = lax.axis_size("panel")
    count, size, _ = inverses.shape
    rows, columns = probes.shape
    width = WIDTH if columns % WIDTH == 0 else columns
    chunks = columns // width
    flat = rows % 128 == 0
    if not flat:
        lower_factor = lower_factor.reshape(rows, panels, rows).transpose(1, 0, 2)
    bf16, f32 = jnp.bfloat16, jnp.float32
    dma = pltpu.SemaphoreType.DMA
    return pl.pallas_call(
        functools.partial(kernel, panels, width, flat),
        out_shape=pltpu.VMEM((rows, columns), f32),
        in_specs=[pl.BlockSpec(memory_space=pltpu.HBM)] * 3,
        out_specs=pl.BlockSpec(memory_space=pltpu.VMEM),
        scratch_shapes=[
            pltpu.VMEM((panels, rows, rows), bf16),
            pltpu.VMEM((count, size, size), f32),
            pltpu.VMEM((count, size, size), bf16),
            pltpu.VMEM((count, size, size), bf16),
            pltpu.VMEM((panels * count, rows, size), bf16),
            pltpu.VMEM((panels * count, rows, size), bf16),
            pltpu.VMEM((rows, columns), bf16),
            pltpu.VMEM((chunks, panels * rows, width), bf16),
            pltpu.VMEM((rows, width), f32),
            dma((2,)),
            dma((panels,)),
            dma((chunks, panels * count)),
            dma((chunks, panels * count)),
        ],
        compiler_params=pltpu.CompilerParams(
            collective_id=0, has_side_effects=True, vmem_limit_bytes=54 * 1024 * 1024
        ),
    )(lower_factor, inverses, probes)


def solution(mesh):
    return jax.shard_map(
        per_device,
        mesh=mesh,
        in_specs=(
            P(("expert", "panel"), None),
            P(("expert", "panel"), None, None),
            P(("expert", "panel"), None),
        ),
        out_specs=P(("expert", "panel"), None),
        check_vma=False,
    )
```

```python
import functools

import jax
import jax.numpy as jnp
from jax import lax
from jax.experimental import pallas as pl
from jax.experimental.pallas import tpu as pltpu
from jax.sharding import PartitionSpec as P

MESH = pl.DeviceIdType.MESH
WIDTH = 256


def dot(a, b):
    return jnp.dot(a, b, preferred_element_type=jnp.float32)


def split(x):
    high = x.astype(jnp.bfloat16)
    return high, (x - high.astype(jnp.float32)).astype(jnp.bfloat16)


def kernel(
    panels, width, flat, lower, inverses, probes, out,
    factor, inverse, inv_high, inv_low, folded, probe, solved, pending,
    load_sem, factor_sem, send_sem, recv_sem,
):
    count, size = inverses.shape[0], inverses.shape[1]
    rows = count * size
    chunks = probes.shape[1] // width
    me = lax.axis_index("panel")
    after = lax.rem(me + 1, panels)
    has_next = me < panels - 1
    blocks = [slice(b * size, (b + 1) * size) for b in range(count)]

    barrier = pltpu.get_barrier_semaphore()

    @pl.when(me > 0)
    def _():
        pl.semaphore_signal(barrier, inc=1, device_id={"panel": me - 1}, device_id_type=MESH)

    def load_factor(q):
        if flat:
            source = lower.at[:, pl.ds(pl.multiple_of(q * rows, 128), rows)]
        else:
            source = lower.at[q]
        return pltpu.make_async_copy(source, factor.at[q], factor_sem.at[q])

    def block_copy(c, g):
        block = solved.at[c, pl.ds(pl.multiple_of(g * size, 16), size)]
        return pltpu.make_async_remote_copy(
            src_ref=block,
            dst_ref=block,
            send_sem=send_sem.at[c, g],
            recv_sem=recv_sem.at[c, g],
            device_id={"panel": after},
            device_id_type=MESH,
        )

    def send(c, g):
        @pl.when(has_next)
        def _():
            block_copy(c, g).start()

    def columns_of(c):
        return pl.ds(pl.multiple_of(c * width, 128), width)

    def begin(c):
        for b in range(count):
            given = probe[blocks[b], columns_of(c)]
            pending[blocks[b]] = dot(inv_high[b], given) + dot(inv_low[b], given)

    def fold(q, j, first):
        for b in range(first, count):
            part = factor[q, blocks[b], blocks[j]]
            g = q * count + j
            folded[g, blocks[b]] = (dot(inv_high[b], part) + dot(inv_low[b], part)).astype(jnp.bfloat16)

    def update(c, g, first):
        block = solved[c, pl.ds(pl.multiple_of(g * size, 16), size)]
        below = slice(first * size, rows)
        pending[below] -= dot(folded[g, below], block)

    def finalize(c, b):
        block = pending[blocks[b]]
        g = me * count + b
        solved[c, pl.ds(pl.multiple_of(g * size, 16), size)] = block.astype(jnp.bfloat16)
        send(c, g)
        out[blocks[b], columns_of(c)] = block

    load_inverse = pltpu.make_async_copy(inverses, inverse, load_sem.at[0])
    load_probe = pltpu.make_async_copy(probes, probe, load_sem.at[1])
    load_inverse.start()
    load_probe.start()
    load_factor(me).start()

    def start_factor(q, carry):
        load_factor(q).start()
        return carry

    lax.fori_loop(0, me, start_factor, 0)
    load_inverse.wait()
    for b in range(count):
        inv_high[b], inv_low[b] = split(inverse[b])
    load_probe.wait()
    begin(0)

    @pl.when(has_next)
    def _():
        pl.semaphore_wait(barrier, 1)

    @pl.when(me == 0)
    def _():
        finalize(0, 0)

    load_factor(me).wait()
    for j in range(count - 1):
        fold(me, j, j + 1)

    def chunk(c, carry):
        @pl.when(c > 0)
        def _():
            begin(c)

        def earlier(q, carry):
            @pl.when(c == 0)
            def _():
                load_factor(q).wait()

            for j in range(count):
                g = q * count + j
                block_copy(c, g).wait_recv()
                send(c, g)

                @pl.when(c == 0)
                def _():
                    fold(q, j, 0)

                update(c, g, 0)
            return carry

        lax.fori_loop(0, me, earlier, 0)

        @pl.when(me + c > 0)
        def _():
            finalize(c, 0)

        for b in range(1, count):
            update(c, me * count + b - 1, b)
            finalize(c, b)
        return carry

    lax.fori_loop(0, chunks, chunk, 0)

    def finish(c, carry):
        @pl.when(has_next)
        def _():
            def sent(g, carry):
                block_copy(c, g).wait_send()
                return carry

            lax.fori_loop(0, (me + 1) * count, sent, 0)

        return carry

    lax.fori_loop(0, chunks, finish, 0)


def per_device(lower_factor, inverses, probes):
    panels = lax.axis_size("panel")
    count, size, _ = inverses.shape
    rows, columns = probes.shape
    width = WIDTH if columns % WIDTH == 0 else columns
    chunks = columns // width
    flat = rows % 128 == 0
    if not flat:
        lower_factor = lower_factor.reshape(rows, panels, rows).transpose(1, 0, 2)
    bf16, f32 = jnp.bfloat16, jnp.float32
    dma = pltpu.SemaphoreType.DMA
    return pl.pallas_call(
        functools.partial(kernel, panels, width, flat),
        out_shape=pltpu.VMEM((rows, columns), f32),
        in_specs=[pl.BlockSpec(memory_space=pltpu.HBM)] * 3,
        out_specs=pl.BlockSpec(memory_space=pltpu.VMEM),
        scratch_shapes=[
            pltpu.VMEM((panels, rows, rows), bf16),
            pltpu.VMEM((count, size, size), f32),
            pltpu.VMEM((count, size, size), bf16),
            pltpu.VMEM((count, size, size), bf16),
            pltpu.VMEM((panels * count, rows, size), bf16),
            pltpu.VMEM((rows, columns), bf16),
            pltpu.VMEM((chunks, panels * rows, width), bf16),
            pltpu.VMEM((rows, width), f32),
            dma((2,)),
            dma((panels,)),
            dma((chunks, panels * count)),
            dma((chunks, panels * count)),
        ],
        compiler_params=pltpu.CompilerParams(
            collective_id=0, has_side_effects=True, vmem_limit_bytes=54 * 1024 * 1024
        ),
    )(lower_factor, inverses, probes)


def solution(mesh):
    return jax.shard_map(
        per_device,
        mesh=mesh,
        in_specs=(
            P(("expert", "panel"), None),
            P(("expert", "panel"), None, None),
            P(("expert", "panel"), None),
        ),
        out_specs=P(("expert", "panel"), None),
        check_vma=False,
    )
```
